32 devices in a mesh: cases: 2 (over y), wheel: 4 (over z), inst: 4 (over x, core).
Axes of the slice: x: 2, y: 2, z: 4, core: 2. Of those that a mesh axis runs over, the one named last changes fastest.
Arguments:
- state: float32 [16, 5, 1024, 128], P('inst', None, ('cases', 'wheel')), parts along dimension 2, as said below
- slot_blade: int32 [8], P(('cases', 'wheel')), parts along dimension 0, may hold values from 0 to 3, each once
- blade_class: int32 [8], P('cases'), parts along dimension 0, may hold values from 0 to 3
- face_index: int32 [8, 2, 128], P(('cases', 'wheel')), parts along dimension 0, may hold values from 0 to 127, as said below
- class_amplitude: float32 [4], replicated, may hold values from 0.3 to 1.2
- class_phase: float32 [4], replicated, may hold values from -3.140625 to 3.140625
Outputs:
- new_state: float32 [16, 5, 1024, 128], P('inst', None, ('cases', 'wheel')), parts along dimension 2
- last_residual: float32 [16, 5, 1024, 128], P('inst', None, ('cases', 'wheel')), parts along dimension 2
The draws below stay inside these ranges and needn't reach their ends.
There are 2 independent parts, one for each index of `cases`. The reference program is written for one: setup_inputs(seed, part) draws one part's arguments, and reference() takes and returns one part's arrays. A program takes and returns all parts, laid end to end along the dimension named above; an argument that names none is the same for every part. Nothing has to cross between parts.
Inputs may be any that keep to these rules, and one draw needn't show every extreme that they name: `state`: density lies in [0.8, 1.2] and pressure is positive in every cell. `slot_blade`: each blade sits in exactly one slot. face_index[s, side, k] differs from k by at most one.
All inputs are finite; a program needn't handle non-finite values.
Results may differ from the reference program's by a relative error of at most 0.0003.
Values sent between devices are 32-bit elements; how exact they have to be, the bound alone decides.
A program may use at most 64 MiB of HBM per device.

```python
import math
import jax
import jax.numpy as jnp
from jax import lax

INST = 16
NVAR = 5
NCLASS = 4
CT = 128
CX = 128
PASS = 4


def draw_state(key, part):
    grid_shape = (INST, PASS * CT, CX)
    subkeys = jax.random.split(key, 5)
    noises = [jnp.clip(jax.random.normal(subkey, grid_shape, jnp.float32), -2.0, 2.0) for subkey in subkeys]
    density = 1.0 + 0.1 * noises[0]
    axial_vel = 0.5 + 0.2 * noises[1]
    pitch_vel = 0.2 * noises[2]
    radial_vel = 0.1 * noises[3]
    pressure = 1.0 / 1.4 * (1.0 + 0.1 * noises[4])
    energy = pressure / 0.4 + 0.5 * density * (axial_vel * axial_vel + pitch_vel * pitch_vel + radial_vel * radial_vel)
    stacked = jnp.stack([density, density * axial_vel, density * pitch_vel, density * radial_vel, energy], 1)
    return stacked.astype(jnp.float32)


def draw_face_index(key, part):
    base_cells = jnp.arange(CX, dtype=jnp.int32)[None, None, :]
    offsets = jax.random.randint(key, (PASS, 2, CX), -1, 2)
    return jnp.clip(base_cells + offsets, 0, CX - 1).astype(jnp.int32)


def place_ends(entries, rng, low, high):
    spot = [jax.random.randint(jax.random.fold_in(rng, axis), (), 0, length) for axis, length in enumerate(entries.shape)]
    longest = entries.shape.index(max(entries.shape))
    next_to = spot[:longest] + [(spot[longest] + 1) % entries.shape[longest]] + spot[longest + 1:]
    return entries.at[tuple(spot)].set(low).at[tuple(next_to)].set(high)


def setup_inputs(seed: int = 0, part: int = 0) -> dict:
    keys = jax.random.split(jax.random.key(seed), 7)
    part_splits = jax.random.split(jax.random.fold_in(keys[6], part), 7)
    state = draw_state(jax.random.fold_in(jax.random.fold_in(keys[6], part), 71), part)
    slot_blade = jax.random.permutation(part_splits[1], PASS).astype(jnp.int32)
    blade_class = place_ends(jax.random.randint(part_splits[2], (PASS,), 0, NCLASS), jax.random.fold_in(part_splits[2], 1), 0, NCLASS - 1).astype(jnp.int32)
    face_index = draw_face_index(jax.random.fold_in(jax.random.fold_in(keys[6], part), 71), part)
    class_amplitude = jnp.clip(jnp.exp(jax.random.uniform(keys[4], (NCLASS,), jnp.float32, math.log(0.3), math.log(1.2))), 0.3, 1.2)
    class_phase = jnp.clip(jax.random.uniform(keys[5], (NCLASS,), jnp.float32, -3.140625, 3.140625), -3.140625, 3.140625)
    return {"state": state, "slot_blade": slot_blade, "blade_class": blade_class, "face_index": face_index, "class_amplitude": class_amplitude, "class_phase": class_phase}


HEAT_RATIO = 1.4
TIME_STEP = 0.05
DISSIPATION = 2.0
FREQUENCY = 0.5


def fluxes(field):
    density = field[:, 0]
    axial_mom = field[:, 1]
    pitch_mom = field[:, 2]
    radial_mom = field[:, 3]
    energy = field[:, 4]
    inverse = 1.0 / density
    axial_vel = axial_mom * inverse
    pitch_vel = pitch_mom * inverse
    pressure = (HEAT_RATIO - 1.0) * (energy - 0.5 * (axial_mom * axial_mom + pitch_mom * pitch_mom + radial_mom * radial_mom) * inverse)
    enthalpy = energy + pressure
    axial_flux = jnp.stack([axial_mom, axial_mom * axial_vel + pressure, pitch_mom * axial_vel, radial_mom * axial_vel, enthalpy * axial_vel], 1)
    pitch_flux = jnp.stack([pitch_mom, axial_mom * pitch_vel, pitch_mom * pitch_vel + pressure, radial_mom * pitch_vel, enthalpy * pitch_vel], 1)
    return axial_flux, pitch_flux


def spectral_matrix(count):
    steps_apart = (jnp.arange(count)[:, None] - jnp.arange(count)[None, :]).astype(jnp.int32)
    apart = steps_apart != 0
    angle = jnp.where(apart, (math.pi / count) * steps_apart.astype(jnp.float32), 1.0)
    parity = jnp.where(steps_apart % 2 == 0, 1.0, -1.0)
    return jnp.where(apart, 0.5 * parity * jnp.cos(angle) / jnp.sin(angle), 0.0).astype(jnp.float32)


def face_terms(left, right, flux_left, flux_right, speed):
    return 0.5 * (flux_left + flux_right) - speed * 0.5 * (left + right) - 0.5 * DISSIPATION * (right - left)


def residual_of(field, speed, face_index, matrix):
    last_rows = jnp.roll(field[:, :, :, -1, :], 1, axis=2)
    first_rows = jnp.roll(field[:, :, :, 0, :], -1, axis=2)
    row_shape = last_rows.shape
    lower = jnp.take_along_axis(last_rows, jnp.broadcast_to(face_index[:, 0, :], row_shape), axis=3)
    upper = jnp.take_along_axis(first_rows, jnp.broadcast_to(face_index[:, 1, :], row_shape), axis=3)
    extended = jnp.concatenate([lower[:, :, :, None, :], field, upper[:, :, :, None, :]], axis=3)
    axial_ext, pitch_ext = fluxes(extended)
    axial_flux = axial_ext[:, :, :, 1:-1, :]
    axial_pad = jnp.concatenate([axial_flux[..., :1], axial_flux, axial_flux[..., -1:]], axis=4)
    field_pad = jnp.concatenate([field[..., :1], field, field[..., -1:]], axis=4)
    axial_face = face_terms(field_pad[..., :-1], field_pad[..., 1:], axial_pad[..., :-1], axial_pad[..., 1:], 0.0)
    pitch_face = face_terms(extended[:, :, :, :-1], extended[:, :, :, 1:], pitch_ext[:, :, :, :-1], pitch_ext[:, :, :, 1:], speed[:, None, :, None, None])
    spectral = jnp.einsum('nm,mvpjk->nvpjk', matrix, field, precision=lax.Precision.HIGHEST)
    return -(axial_face[..., 1:] - axial_face[..., :-1]) - (pitch_face[:, :, :, 1:] - pitch_face[:, :, :, :-1]) - FREQUENCY * spectral


def reference(state, slot_blade, blade_class, face_index, class_amplitude, class_phase):
    passages = slot_blade.shape[0]
    field = state.reshape(INST, NVAR, passages, CT, CX)
    classes = blade_class[slot_blade]
    amplitude = class_amplitude[classes]
    phase = class_phase[classes]
    instance = jnp.arange(INST).astype(jnp.float32)
    speed = amplitude[None, :] * jnp.sin((2.0 * math.pi / INST) * instance[:, None] + phase[None, :])
    matrix = spectral_matrix(INST)
    first = field + (0.5 * TIME_STEP) * residual_of(field, speed, face_index, matrix)
    last_residual = residual_of(first, speed, face_index, matrix)
    new_state = field + TIME_STEP * last_residual
    return new_state.reshape(state.shape), last_residual.reshape(state.shape)
```

```python
import functools
import math

import jax
import jax.numpy as jnp
from jax import lax
from jax.experimental import pallas as pl
from jax.experimental.pallas import tpu as pltpu
from jax.sharding import PartitionSpec as P

TIME_STEP = 0.05
GAMMA1 = 0.4
FREQUENCY = 0.5
NV = 5
MESH = pl.DeviceIdType.MESH


def flip(i, off):
    out, b = i, 1
    while b <= off:
        if off & b:
            out = out + b - 2 * b * ((i // b) % 2)
        b *= 2
    return out


def spectral(q):
    s = [q[i] + q[i + 8] for i in range(8)]
    d = [q[i] - q[i + 8] for i in range(8)]
    c = [0.5 * (-1) ** k / math.tan(math.pi * k / 8) for k in range(1, 4)]
    t = [0.5 * (-1) ** k / math.sin(math.pi * k / 8) for k in range(1, 4)]
    s2 = [s[i] - s[(i + 2) % 8] for i in range(8)]
    s4 = [s[i] - s[i + 4] for i in range(4)]

    def dd(i):
        i %= 16
        return (d[i], 1) if i < 8 else (d[i - 8], -1)

    cache = {}

    def ddiff(i, j):
        (x, sx), (y, sy) = dd(i), dd(j)
        key = (i % 8, j % 8, sx * sy)
        if key not in cache:
            cache[key] = x - y if sx * sy > 0 else x + y
        return cache[key], sx

    out = [None] * 16
    for n in range(8):
        a1 = s2[(n - 1) % 8]
        a3 = s2[(n + 3) % 8]
        i = (n - 2) % 8
        a2 = s4[i] * c[1] if i < 4 else s4[i - 4] * (-c[1])
        u = c[0] * a1 - c[2] * a3 + a2
        w = None
        for k in (1, 2, 3):
            v, sg = ddiff(n - k, n + k)
            term = v * (sg * t[k - 1])
            w = term if w is None else w + term
        x, sg = dd(n - 4)
        w = w + x * (0.5 * sg)
        out[n] = u + w
        out[n + 8] = u - w
    return out


def shift(x, k, axis):
    size = x.shape[axis]
    return pltpu.roll(x, k % size, axis)


def kernel(n_i, n_w, per, rows, state, slot_blade, blade_class, amp, phase, face, res,
           qx, fx, rs, spd, own_sem, snd_m, rcv_m, snd_h, rcv_h, snd_f, rcv_f, snd_r, rcv_r):
    me = lax.axis_index("inst")
    w = lax.axis_index("wheel")
    up_w, dn_w = lax.rem(w + 1, n_w), lax.rem(w + n_w - 1, n_w)
    ct = rows * n_i
    inst = n_i * per
    ext = rows + 8

    def dev(wheel, i):
        return {"wheel": wheel, "inst": i}

    barrier = pltpu.get_barrier_semaphore()
    for off in range(1, n_i):
        pl.semaphore_signal(barrier, inc=1, device_id=dev(w, flip(me, off)), device_id_type=MESH)

    @pl.when(me == 0)
    def _():
        for j in range(n_i):
            pl.semaphore_signal(barrier, inc=1, device_id=dev(dn_w, j), device_id_type=MESH)

    @pl.when(me == n_i - 1)
    def _():
        for j in range(n_i):
            pl.semaphore_signal(barrier, inc=1, device_id=dev(up_w, j), device_id_type=MESH)

    mine = pl.ds(me * per, per)
    own_copy = pltpu.make_async_copy(
        state.at[:, :, pl.ds(me * rows, rows), :], qx.at[mine, :, pl.ds(0, rows), :], own_sem.at[0])
    own_copy.start()
    cls = blade_class[slot_blade[0]]
    instance = lax.broadcasted_iota(jnp.int32, (inst, 128), 0).astype(jnp.float32)
    spd[...] = amp[cls] * jnp.sin((2.0 * math.pi / inst) * instance + phase[cls])
    lane = lax.broadcasted_iota(jnp.int32, (8, 128), 1)
    sub = lax.broadcasted_iota(jnp.int32, (8, 128), 0)
    lo_idx = jnp.where(me == 0, face[0, 0:1, :], lane[0:1])
    hi_idx = jnp.where(me == n_i - 1, face[0, 1:2, :], lane[0:1])
    offs = jnp.where(sub == 0, hi_idx, jnp.where(sub == 7, lo_idx, lane)) - lane

    pl.semaphore_wait(barrier, n_i + 1)

    def halo(side, i):
        if side == 0:
            row, slot, wheel = (rows * i - 1) % ct, ext - 1, (up_w if i == 0 else w)
            far = i == 0
        else:
            row, slot, wheel = (rows * (i + 1)) % ct, rows, (dn_w if i == n_i - 1 else w)
            far = i == n_i - 1
        src = state.at[:, :, pl.ds(row, 1), :]
        dst = qx.at[mine, :, pl.ds(slot, 1), :]
        remote = pltpu.make_async_remote_copy(
            src, dst, snd_h.at[side, i], rcv_h.at[side, me], device_id=dev(wheel, i), device_id_type=MESH)
        local = pltpu.make_async_copy(src, dst, rcv_h.at[side, me])
        return far, remote, local

    for side in range(2):
        for i in range(n_i):
            far, remote, local = halo(side, i)
            if far:
                remote.start()
            else:
                @pl.when(me != i)
                def _(remote=remote):
                    remote.start()

                @pl.when(me == i)
                def _(local=local):
                    local.start()

    def main(off):
        to = flip(me, off)
        return pltpu.make_async_remote_copy(
            state.at[:, :, pl.ds(to * rows, rows), :], qx.at[mine, :, pl.ds(0, rows), :],
            snd_m.at[off], rcv_m.at[off], device_id=dev(w, to), device_id_type=MESH)

    order_out = list(range(2, n_i)) + [1]
    for off in order_out:
        main(off).start()

    first_lane = lax.broadcasted_iota(jnp.int32, (rows, 128), 1) == 0
    last_lane = lax.broadcasted_iota(jnp.int32, (rows, 128), 1) == 127

    def flux_part(buf, n):
        halo_q = []
        for v in range(NV):
            x = buf[n, v, pl.ds(rows, 8), :]
            halo_q.append(jnp.where(offs == 0, x, jnp.where(offs == 1, shift(x, -1, 1), shift(x, 1, 1))))
        q = [jnp.concatenate([buf[n, v, pl.ds(0, rows), :], halo_q[v]], axis=0) for v in range(NV)]
        rho, mx, mt, mr, en = q
        inv = 1.0 / rho
        ux, ut = mx * inv, mt * inv
        p = GAMMA1 * (en - 0.5 * (mx * ux + mt * ut + mr * mr * inv))
        h = en + p
        speed = spd[pl.ds(n, 1), :]
        hux = 0.5 * ux[:rows]
        hut = 0.5 * ut
        hrel = hut - 0.5 * speed
        hp = 0.5 * p
        out = []
        for v in range(NV):
            base = h if v == 4 else q[v]
            g = base[:rows] * hux
            f = q[v] * hrel
            if v == 1:
                g = g + hp[:rows]
            if v == 2:
                f = f + hp
            if v == 4:
                f = f + p * hut
            qc = q[v][:rows]
            a_ax, b_ax = g - qc, g + qc
            right = jnp.where(last_lane, a_ax, shift(a_ax, -1, 1))
            left = jnp.where(first_lane, b_ax, shift(b_ax, 1, 1))
            above = shift(f - q[v], -1, 0)[:rows]
            below = shift(f + q[v], 1, 0)[:rows]
            out.append((left - right) + (below - above) - 4.0 * qc)
        return out

    def wait_halo(side, j):
        dst = qx.at[pl.ds(j * per, per), :, pl.ds(rows if side else ext - 1, 1), :]
        pltpu.make_async_copy(state.at[:, :, pl.ds(0, 1), :], dst, rcv_h.at[side, j]).wait()

    for off in range(n_i):
        j = flip(me, off)
        if off == 0:
            own_copy.wait()
        else:
            pltpu.make_async_copy(
                state.at[:, :, pl.ds(0, rows), :], qx.at[pl.ds(j * per, per), :, pl.ds(0, rows), :],
                rcv_m.at[off]).wait()
        wait_halo(0, j)
        wait_halo(1, j)

        @pl.loop(0, per)
        def _(k, j=j):
            n = j * per + k
            part = flux_part(qx, n)
            for v in range(NV):
                fx[n, v, pl.ds(0, rows), :] = qx[n, v, pl.ds(0, rows), :] + (0.5 * TIME_STEP) * part[v]

    def spectral_first(t):
        @pl.loop(0, NV)
        def _(v):
            sp = spectral([qx[n, v, pl.ds(8 * t, 8), :] for n in range(inst)])
            for n in range(inst):
                fx[n, v, pl.ds(8 * t, 8), :] += (-0.5 * TIME_STEP * FREQUENCY) * sp[n]

    def spectral_last(t):
        @pl.loop(0, NV)
        def _(v):
            sp = spectral([fx[n, v, pl.ds(8 * t, 8), :] for n in range(inst)])
            for n in range(inst):
                rs[n, v, pl.ds(8 * t, 8), :] = -FREQUENCY * sp[n]

    tiles = rows // 8
    edge = sorted({0, tiles - 1})
    inner = [t for t in range(tiles) if t not in edge]
    for t in edge:
        spectral_first(t)

    above_dev = dev(jnp.where(me == n_i - 1, up_w, w), lax.rem(me + 1, n_i))
    below_dev = dev(jnp.where(me == 0, dn_w, w), lax.rem(me + n_i - 1, n_i))
    to_above = pltpu.make_async_remote_copy(
        fx.at[:, :, pl.ds(rows - 1, 1), :], fx.at[:, :, pl.ds(ext - 1, 1), :],
        snd_f.at[0], rcv_f.at[0], device_id=above_dev, device_id_type=MESH)
    to_below = pltpu.make_async_remote_copy(
        fx.at[:, :, pl.ds(0, 1), :], fx.at[:, :, pl.ds(rows, 1), :],
        snd_f.at[1], rcv_f.at[1], device_id=below_dev, device_id_type=MESH)
    to_above.start()
    to_below.start()
    for t in inner:
        spectral_first(t)
    for t in range(tiles):
        spectral_last(t)
    to_above.wait_recv()
    to_below.wait_recv()

    def back(off):
        to = flip(me, off)
        return pltpu.make_async_remote_copy(
            rs.at[pl.ds(to * per, per)], res.at[:, :, pl.ds(me * rows, rows), :],
            snd_r.at[off], rcv_r.at[off], device_id=dev(w, to), device_id_type=MESH)

    own_back = pltpu.make_async_copy(rs.at[mine], res.at[:, :, pl.ds(me * rows, rows), :], own_sem.at[1])
    for off in order_out + [0]:
        j = flip(me, off)

        @pl.loop(0, per)
        def _(k, j=j):
            n = j * per + k
            part = flux_part(fx, n)
            for v in range(NV):
                rs[n, v] += part[v]

        if off == 0:
            own_back.start()
        else:
            back(off).start()

    own_back.wait()
    for off in range(1, n_i):
        main(off).wait_send()
    for side in range(2):
        for i in range(n_i):
            far, remote, local = halo(side, i)
            if far:
                remote.wait_send()
            else:
                @pl.when(me != i)
                def _(remote=remote):
                    remote.wait_send()
    to_above.wait_send()
    to_below.wait_send()
    for off in order_out:
        j = flip(me, off)
        back(off).wait_send()
        pltpu.make_async_copy(rs.at[mine], res.at[:, :, pl.ds(j * rows, rows), :], rcv_r.at[off]).wait()


def body(n_i, n_w, state, slot_blade, blade_class, face_index, amp, phase):
    per, nv, ct, cx = state.shape
    rows = ct // n_i
    inst = per * n_i
    smem = pl.BlockSpec(memory_space=pltpu.SMEM)
    dma = pltpu.SemaphoreType.DMA
    last = pl.pallas_call(
        functools.partial(kernel, n_i, n_w, per, rows),
        out_shape=jax.ShapeDtypeStruct(state.shape, jnp.float32),
        in_specs=[pl.BlockSpec(memory_space=pl.ANY), smem, smem, smem, smem,
                  pl.BlockSpec(memory_space=pltpu.VMEM)],
        out_specs=pl.BlockSpec(memory_space=pl.ANY),
        scratch_shapes=[
            pltpu.VMEM((inst, nv, rows + 8, cx), jnp.float32),
            pltpu.VMEM((inst, nv, rows + 8, cx), jnp.float32),
            pltpu.VMEM((inst, nv, rows, cx), jnp.float32),
            pltpu.VMEM((inst, cx), jnp.float32),
            dma((2,)),
            dma((n_i,)), dma((n_i,)),
            dma((2, n_i)), dma((2, n_i)),
            dma((2,)), dma((2,)),
            dma((n_i,)), dma((n_i,)),
        ],
        compiler_params=pltpu.CompilerParams(
            collective_id=0, has_side_effects=True, vmem_limit_bytes=48 * 1024 * 1024),
        cost_estimate=pl.CostEstimate(flops=50_000_000, bytes_accessed=2_700_000, transcendentals=0),
    )(state, slot_blade, blade_class, amp, phase, face_index)
    return state + TIME_STEP * last, last


def solution(mesh):
    placed = (
        P("inst", None, ("cases", "wheel"), None),
        P(("cases", "wheel")),
        P("cases"),
        P(("cases", "wheel"), None, None),
        P(),
        P(),
    )
    return jax.shard_map(
        functools.partial(body, mesh.shape["inst"], mesh.shape["wheel"]),
        mesh=mesh,
        in_specs=placed,
        out_specs=(
            P("inst", None, ("cases", "wheel"), None),
            P("inst", None, ("cases", "wheel"), None),
        ),
        check_vma=False,
    )
```

```python
import functools
import math

import jax
import jax.numpy as jnp
from jax import lax
from jax.experimental import pallas as pl
from jax.experimental.pallas import tpu as pltpu
from jax.sharding import PartitionSpec as P

TIME_STEP = 0.05
GAMMA1 = 0.4
FREQUENCY = 0.5
NV = 5
MESH = pl.DeviceIdType.MESH


def flip(i, off):
    out, b = i, 1
    while b <= off:
        if off & b:
            out = out + b - 2 * b * ((i // b) % 2)
        b *= 2
    return out


def spectral(q):
    s = [q[i] + q[i + 8] for i in range(8)]
    d = [q[i] - q[i + 8] for i in range(8)]
    c = [0.5 * (-1) ** k / math.tan(math.pi * k / 8) for k in range(1, 4)]
    t = [0.5 * (-1) ** k / math.sin(math.pi * k / 8) for k in range(1, 4)]
    s2 = [s[i] - s[(i + 2) % 8] for i in range(8)]
    s4 = [s[i] - s[i + 4] for i in range(4)]

    def dd(i):
        i %= 16
        return (d[i], 1) if i < 8 else (d[i - 8], -1)

    cache = {}

    def ddiff(i, j):
        (x, sx), (y, sy) = dd(i), dd(j)
        key = (i % 8, j % 8, sx * sy)
        if key not in cache:
            cache[key] = x - y if sx * sy > 0 else x + y
        return cache[key], sx

    out = [None] * 16
    for n in range(8):
        a1 = s2[(n - 1) % 8]
        a3 = s2[(n + 3) % 8]
        i = (n - 2) % 8
        a2 = s4[i] * c[1] if i < 4 else s4[i - 4] * (-c[1])
        u = c[0] * a1 - c[2] * a3 + a2
        w = None
        for k in (1, 2, 3):
            v, sg = ddiff(n - k, n + k)
            term = v * (sg * t[k - 1])
            w = term if w is None else w + term
        x, sg = dd(n - 4)
        w = w + x * (0.5 * sg)
        out[n] = u + w
        out[n + 8] = u - w
    return out


def shift(x, k, axis):
    size = x.shape[axis]
    return pltpu.roll(x, k % size, axis)


def kernel(n_i, n_w, per, rows, state, slot_blade_h, blade_class_h, amp_h, phase_h, face_h, new, res,
           st, qx, fx, eb, rs, spd, slot_blade, blade_class, amp, phase, face, par_sem, own_sem,
           snd_m, rcv_m, snd_h, rcv_h, snd_f, rcv_f, snd_r, rcv_r):
    me = lax.axis_index("inst")
    w = lax.axis_index("wheel")
    up_w, dn_w = lax.rem(w + 1, n_w), lax.rem(w + n_w - 1, n_w)
    ct = rows * n_i
    inst = n_i * per
    tiles = rows // 8
    arrivals = [0] + ([tiles - 1] if tiles > 1 else []) + list(range(1, tiles - 1))

    def dev(wheel, i):
        return {"wheel": wheel, "inst": i}

    small = [(slot_blade_h, slot_blade), (blade_class_h, blade_class), (amp_h, amp), (phase_h, phase), (face_h, face)]
    for i, (a, b) in enumerate(small):
        pltpu.make_async_copy(a, b, par_sem.at[i]).start()

    barrier = pltpu.get_barrier_semaphore()
    for off in range(1, n_i):
        pl.semaphore_signal(barrier, inc=1, device_id=dev(w, flip(me, off)), device_id_type=MESH)

    @pl.when(me == 0)
    def _():
        for j in range(n_i):
            pl.semaphore_signal(barrier, inc=1, device_id=dev(dn_w, j), device_id_type=MESH)

    @pl.when(me == n_i - 1)
    def _():
        for j in range(n_i):
            pl.semaphore_signal(barrier, inc=1, device_id=dev(up_w, j), device_id_type=MESH)

    mine = pl.ds(me * per, per)
    own_copy = pltpu.make_async_copy(
        state.at[:, :, pl.ds(me * rows, rows), :], qx.at[mine, :, pl.ds(0, rows), :], own_sem.at[0])
    own_copy.start()
    st_copy = pltpu.make_async_copy(state, st, own_sem.at[1])
    for i, (a, b) in enumerate(small):
        pltpu.make_async_copy(a, b, par_sem.at[i]).wait()
    cls = blade_class[slot_blade[0]]
    instance = lax.broadcasted_iota(jnp.int32, (inst, 128), 0).astype(jnp.float32)
    spd[...] = amp[cls] * jnp.sin((2.0 * math.pi / inst) * instance + phase[cls])
    lane = lax.broadcasted_iota(jnp.int32, (8, 128), 1)
    sub = lax.broadcasted_iota(jnp.int32, (8, 128), 0)
    lo_idx = jnp.where(me == 0, face[0, 0:1, :], lane[0:1])
    hi_idx = jnp.where(me == n_i - 1, face[0, 1:2, :], lane[0:1])
    offs = jnp.where(sub == 0, hi_idx, jnp.where(sub == 7, lo_idx, lane)) - lane
    top = sub < 4
    first_lane, last_lane = lane == 0, lane == 127

    pl.semaphore_wait(barrier, n_i + 1)

    def halo(side, i):
        if side == 0:
            row, slot, wheel = (rows * i - 1) % ct, rows + 7, (up_w if i == 0 else w)
            far = i == 0
        else:
            row, slot, wheel = (rows * (i + 1)) % ct, rows, (dn_w if i == n_i - 1 else w)
            far = i == n_i - 1
        src = state.at[:, :, pl.ds(row, 1), :]
        dst = qx.at[mine, :, pl.ds(slot, 1), :]
        remote = pltpu.make_async_remote_copy(
            src, dst, snd_h.at[side, i], rcv_h.at[side, me], device_id=dev(wheel, i), device_id_type=MESH)
        local = pltpu.make_async_copy(src, dst, rcv_h.at[side, me])
        return far, remote, local

    for side in range(2):
        for i in range(n_i):
            far, remote, local = halo(side, i)
            if far:
                remote.start()
            else:
                @pl.when(me != i)
                def _(remote=remote):
                    remote.start()

                @pl.when(me == i)
                def _(local=local):
                    local.start()

    def main(off, t):
        to = flip(me, off)
        return pltpu.make_async_remote_copy(
            state.at[:, :, pl.ds(to * rows + 8 * t, 8), :], qx.at[mine, :, pl.ds(8 * t, 8), :],
            snd_m.at[off, t], rcv_m.at[off, t], device_id=dev(w, to), device_id_type=MESH)

    order_out = list(range(2, n_i)) + [1]
    for t in arrivals:
        for off in order_out:
            main(off, t).start()
    st_copy.start()

    def tile(buf, n, v, t):
        return buf[n, v, pl.ds(8 * t, 8), :]

    def flux_part(n, q, z):
        both = [jnp.concatenate([q[v], z[v]], axis=0) for v in range(NV)]
        rho, mx, mt, mr, en = both
        inv = 1.0 / rho
        ux, ut = mx * inv, mt * inv
        p = GAMMA1 * (en - 0.5 * (mx * ux + mt * ut + mr * mr * inv))
        h = en + p
        hux = 0.5 * ux[:8]
        hut = 0.5 * ut
        hrel = hut - 0.5 * spd[pl.ds(n, 1), :]
        hp = 0.5 * p
        out = []
        for v in range(NV):
            g = (h[:8] if v == 4 else q[v]) * hux
            f = both[v] * hrel
            if v == 1:
                g = g + hp[:8]
            if v == 2:
                f = f + hp
            if v == 4:
                f = f + p * hut
            a_ax, b_ax = g - q[v], g + q[v]
            right = jnp.where(last_lane, a_ax, shift(a_ax, -1, 1))
            left = jnp.where(first_lane, b_ax, shift(b_ax, 1, 1))
            a_pi, b_pi = f - both[v], f + both[v]
            above = shift(jnp.where(sub == 0, a_pi[8:], a_pi[:8]), -1, 0)
            below = shift(jnp.where(sub == 7, b_pi[8:], b_pi[:8]), 1, 0)
            out.append((left - right) + (below - above) - 4.0 * q[v])
        return out

    def around(buf, n, t, above=True):
        hi = t + 1 if above else t
        lo = tiles if t == 0 else t - 1
        return [jnp.where(top, tile(buf, n, v, hi), tile(buf, n, v, lo)) for v in range(NV)]

    def match(buf):
        @pl.loop(0, inst)
        def _(n):
            for v in range(NV):
                x = tile(buf, n, v, tiles)
                buf[n, v, pl.ds(rows, 8), :] = jnp.where(
                    offs == 0, x, jnp.where(offs == 1, shift(x, -1, 1), shift(x, 1, 1)))

    def section_one(t, above=True):
        @pl.loop(0, NV)
        def _(v):
            q = [tile(qx, n, v, t) for n in range(inst)]
            sp = spectral(q)
            for n in range(inst):
                fx[n, v, pl.ds(8 * t, 8), :] = q[n] - (0.5 * TIME_STEP * FREQUENCY) * sp[n]

        @pl.loop(0, inst, unroll=4)
        def _(n):
            part = flux_part(n, [tile(qx, n, v, t) for v in range(NV)], around(qx, n, t, above))
            for v in range(NV):
                fx[n, v, pl.ds(8 * t, 8), :] += (0.5 * TIME_STEP) * part[v]

    def edges_one():
        def pick(n, v):
            return jnp.where(top, tile(qx, n, v, 0), tile(qx, n, v, tiles - 1))

        @pl.loop(0, NV)
        def _(v):
            q = [pick(n, v) for n in range(inst)]
            sp = spectral(q)
            for n in range(inst):
                eb[n, v] = q[n] - (0.5 * TIME_STEP * FREQUENCY) * sp[n]

        @pl.loop(0, inst, unroll=4)
        def _(n):
            part = flux_part(n, [pick(n, v) for v in range(NV)], [tile(qx, n, v, tiles) for v in range(NV)])
            for v in range(NV):
                eb[n, v] += (0.5 * TIME_STEP) * part[v]

    def section_two(t):
        @pl.loop(0, NV)
        def _(v):
            sp = spectral([tile(fx, n, v, t) for n in range(inst)])
            for n in range(inst):
                rs[n, v, pl.ds(8 * t, 8), :] = -FREQUENCY * sp[n]

        @pl.loop(0, inst, unroll=4)
        def _(n):
            part = flux_part(n, [tile(fx, n, v, t) for v in range(NV)], around(fx, n, t))
            for v in range(NV):
                rs[n, v, pl.ds(8 * t, 8), :] += part[v]

    def back(off, t):
        to = flip(me, off)
        return pltpu.make_async_remote_copy(
            rs.at[pl.ds(to * per, per), :, pl.ds(8 * t, 8), :], res.at[:, :, pl.ds(me * rows + 8 * t, 8), :],
            snd_r.at[off, t], rcv_r.at[off, t], device_id=dev(w, to), device_id_type=MESH)

    def arrive(t):
        for off in range(1, n_i):
            pltpu.make_async_copy(
                state.at[:, :, pl.ds(0, 8), :], qx.at[pl.ds(flip(me, off) * per, per), :, pl.ds(8 * t, 8), :],
                rcv_m.at[off, t]).wait()

    to_above = pltpu.make_async_remote_copy(
        eb.at[:, :, pl.ds(7, 1), :], fx.at[:, :, pl.ds(rows + 7, 1), :], snd_f.at[0], rcv_f.at[0],
        device_id=dev(jnp.where(me == n_i - 1, up_w, w), lax.rem(me + 1, n_i)), device_id_type=MESH)
    to_below = pltpu.make_async_remote_copy(
        eb.at[:, :, pl.ds(0, 1), :], fx.at[:, :, pl.ds(rows, 1), :], snd_f.at[1], rcv_f.at[1],
        device_id=dev(jnp.where(me == 0, dn_w, w), lax.rem(me + n_i - 1, n_i)), device_id_type=MESH)

    own_copy.wait()
    for side in range(2):
        for j in range(n_i):
            dst = qx.at[pl.ds(j * per, per), :, pl.ds(rows if side else rows + 7, 1), :]
            pltpu.make_async_copy(state.at[:, :, pl.ds(0, 1), :], dst, rcv_h.at[side, j]).wait()
    match(qx)
    for t in sorted({0, tiles - 1}):
        arrive(t)
    edges_one()
    to_above.start()
    to_below.start()

    def ghosts():
        to_above.wait_recv()
        to_below.wait_recv()
        match(fx)

    def finish(t):
        section_two(t)
        for off in order_out:
            back(off, t).start()

    if tiles > 3:
        arrive(1)
        section_one(0)
        section_one(1, above=False)
        ghosts()
        finish(0)
        for t in range(2, tiles - 1):
            arrive(t)
        for t in range(1, tiles):
            section_one(t)
        rest = range(1, tiles)
    else:
        for t in range(1, tiles - 1):
            arrive(t)
        for t in range(tiles):
            section_one(t)
        ghosts()
        rest = range(tiles)
    for t in rest:
        finish(t)

    st_copy.wait()
    for t in range(tiles):
        for off in [0, 1] + list(range(2, n_i)):
            j = flip(me, off)
            at = pl.ds(pl.multiple_of(j * rows + 8 * t, 8), 8)
            if off:
                pltpu.make_async_copy(
                    rs.at[mine, :, pl.ds(8 * t, 8), :], res.at[:, :, at, :], rcv_r.at[off, t]).wait()

            for k in range(per):
                for v in range(NV):
                    if off:
                        r = res[k, v, at, :]
                    else:
                        r = rs[me * per + k, v, pl.ds(8 * t, 8), :]
                        res[k, v, at, :] = r
                    new[k, v, at, :] = st[k, v, at, :] + TIME_STEP * r

    for t in range(tiles):
        for off in range(1, n_i):
            main(off, t).wait_send()
            back(off, t).wait_send()
    for side in range(2):
        for i in range(n_i):
            far, remote, local = halo(side, i)
            if far:
                remote.wait_send()
            else:
                @pl.when(me != i)
                def _(remote=remote):
                    remote.wait_send()
    to_above.wait_send()
    to_below.wait_send()


def place(new_v, res_v, new, res, sem):
    copies = []
    for k in range(new_v.shape[0]):
        copies.append(pltpu.make_async_copy(new_v.at[k], new.at[k], sem.at[0, k]))
        copies.append(pltpu.make_async_copy(res_v.at[k], res.at[k], sem.at[1, k]))
    for c in copies:
        c.start()
    for c in copies:
        c.wait()


def body(n_i, n_w, state, slot_blade, blade_class, face_index, amp, phase):
    per, nv, ct, cx = state.shape
    rows = ct // n_i
    tiles = rows // 8
    inst = per * n_i
    dma = pltpu.SemaphoreType.DMA
    anywhere = pl.BlockSpec(memory_space=pl.ANY)
    in_vmem = pl.BlockSpec(memory_space=pltpu.VMEM)

    def stay(x):
        return pltpu.with_memory_space_constraint(x, pltpu.HBM)

    new_v, res_v = pl.pallas_call(
        functools.partial(kernel, n_i, n_w, per, rows),
        out_shape=[pltpu.VMEM(state.shape, jnp.float32)] * 2,
        in_specs=[anywhere] * 6,
        out_specs=[in_vmem] * 2,
        scratch_shapes=[
            pltpu.VMEM(state.shape, jnp.float32),
            pltpu.VMEM((inst, nv, rows + 8, cx), jnp.float32),
            pltpu.VMEM((inst, nv, rows + 8, cx), jnp.float32),
            pltpu.VMEM((inst, nv, 8, cx), jnp.float32),
            pltpu.VMEM((inst, nv, rows, cx), jnp.float32),
            pltpu.VMEM((inst, cx), jnp.float32),
            pltpu.SMEM(slot_blade.shape, jnp.int32),
            pltpu.SMEM(blade_class.shape, jnp.int32),
            pltpu.SMEM(amp.shape, jnp.float32),
            pltpu.SMEM(phase.shape, jnp.float32),
            pltpu.VMEM(face_index.shape, jnp.int32),
            dma((5,)),
            dma((2,)),
            dma((n_i, tiles)), dma((n_i, tiles)),
            dma((2, n_i)), dma((2, n_i)),
            dma((2,)), dma((2,)),
            dma((n_i, tiles)), dma((n_i, tiles)),
        ],
        compiler_params=pltpu.CompilerParams(
            collective_id=0, has_side_effects=True, vmem_limit_bytes=32 * 1024 * 1024),
        cost_estimate=pl.CostEstimate(flops=50_000_000, bytes_accessed=2_700_000, transcendentals=0),
    )(stay(state), slot_blade, stay(blade_class), stay(amp), stay(phase), stay(face_index))
    return pl.pallas_call(
        place,
        out_shape=[jax.ShapeDtypeStruct(state.shape, jnp.float32)] * 2,
        in_specs=[anywhere] * 2,
        out_specs=[anywhere] * 2,
        scratch_shapes=[dma((2, per))],
        cost_estimate=pl.CostEstimate(flops=0, bytes_accessed=5_200_000, transcendentals=0),
    )(*[pltpu.with_memory_space_constraint(x, pltpu.VMEM) for x in (new_v, res_v)])


def solution(mesh):
    placed = (
        P("inst", None, ("cases", "wheel"), None),
        P(("cases", "wheel")),
        P("cases"),
        P(("cases", "wheel"), None, None),
        P(),
        P(),
    )
    return jax.shard_map(
        functools.partial(body, mesh.shape["inst"], mesh.shape["wheel"]),
        mesh=mesh,
        in_specs=placed,
        out_specs=(
            P("inst", None, ("cases", "wheel"), None),
            P("inst", None, ("cases", "wheel"), None),
        ),
        check_vma=False,
    )
```

```python
import functools
import math

import jax
import jax.numpy as jnp
from jax import lax
from jax.experimental import pallas as pl
from jax.experimental.pallas import tpu as pltpu
from jax.sharding import PartitionSpec as P

TIME_STEP = 0.05
GAMMA1 = 0.4
FREQUENCY = 0.5
NV = 5
MESH = pl.DeviceIdType.MESH


def flip(i, off):
    out, b = i, 1
    while b <= off:
        if off & b:
            out = out + b - 2 * b * ((i // b) % 2)
        b *= 2
    return out


def spectral(q):
    s = [q[i] + q[i + 8] for i in range(8)]
    d = [q[i] - q[i + 8] for i in range(8)]
    c = [0.5 * (-1) ** k / math.tan(math.pi * k / 8) for k in range(1, 4)]
    t = [0.5 * (-1) ** k / math.sin(math.pi * k / 8) for k in range(1, 4)]
    s2 = [s[i] - s[(i + 2) % 8] for i in range(8)]
    s4 = [s[i] - s[i + 4] for i in range(4)]

    def dd(i):
        i %= 16
        return (d[i], 1) if i < 8 else (d[i - 8], -1)

    cache = {}

    def ddiff(i, j):
        (x, sx), (y, sy) = dd(i), dd(j)
        key = (i % 8, j % 8, sx * sy)
        if key not in cache:
            cache[key] = x - y if sx * sy > 0 else x + y
        return cache[key], sx

    out = [None] * 16
    for n in range(8):
        a1 = s2[(n - 1) % 8]
        a3 = s2[(n + 3) % 8]
        i = (n - 2) % 8
        a2 = s4[i] * c[1] if i < 4 else s4[i - 4] * (-c[1])
        u = c[0] * a1 - c[2] * a3 + a2
        w = None
        for k in (1, 2, 3):
            v, sg = ddiff(n - k, n + k)
            term = v * (sg * t[k - 1])
            w = term if w is None else w + term
        x, sg = dd(n - 4)
        w = w + x * (0.5 * sg)
        out[n] = u + w
        out[n + 8] = u - w
    return out


def shift(x, k, axis):
    size = x.shape[axis]
    return pltpu.roll(x, k % size, axis)


def kernel(n_i, n_w, per, rows, state, slot_blade_h, blade_class_h, amp_h, phase_h, face_h, new, res,
           st, qx, fx, eb, rs, spd, slot_blade, blade_class, amp, phase, face, par_sem, own_sem,
           joined, around_in, snd_m, rcv_m, snd_h, rcv_h, snd_f, rcv_f, snd_r, rcv_r):
    me = lax.axis_index("inst")
    w = lax.axis_index("wheel")
    up_w, dn_w = lax.rem(w + 1, n_w), lax.rem(w + n_w - 1, n_w)
    ct = rows * n_i
    inst = n_i * per
    tiles = rows // 8
    arrivals = [0] + ([tiles - 1] if tiles > 1 else []) + list(range(1, tiles - 1))

    def dev(wheel, i):
        return {"wheel": wheel, "inst": i}

    small = [(slot_blade_h, slot_blade), (blade_class_h, blade_class), (amp_h, amp), (phase_h, phase), (face_h, face)]
    for i, (a, b) in enumerate(small):
        pltpu.make_async_copy(a, b, par_sem.at[i]).start()

    barrier = pltpu.get_barrier_semaphore()

    @pl.when(me == 0)
    def _():
        for j in range(1, n_i):
            pl.semaphore_signal(barrier, inc=1, device_id=dev(w, j), device_id_type=MESH)

    @pl.when(me != 0)
    def _():
        for j in range(1, n_i):
            @pl.when(me != j)
            def _(j=j):
                pl.semaphore_signal(barrier, inc=1, device_id=dev(w, j), device_id_type=MESH)

    mine = pl.ds(me * per, per)
    own_copy = pltpu.make_async_copy(
        state.at[:, :, pl.ds(me * rows, rows), :], qx.at[mine, :, pl.ds(0, rows), :], own_sem.at[0])
    own_copy.start()
    st_copy = pltpu.make_async_copy(state, st, own_sem.at[1])
    for i, (a, b) in enumerate(small):
        pltpu.make_async_copy(a, b, par_sem.at[i]).wait()
    cls = blade_class[slot_blade[0]]
    instance = lax.broadcasted_iota(jnp.int32, (inst, 128), 0).astype(jnp.float32)
    spd[...] = amp[cls] * jnp.sin((2.0 * math.pi / inst) * instance + phase[cls])
    lane = lax.broadcasted_iota(jnp.int32, (8, 128), 1)
    sub = lax.broadcasted_iota(jnp.int32, (8, 128), 0)
    lo_idx = jnp.where(me == 0, face[0, 0:1, :], lane[0:1])
    hi_idx = jnp.where(me == n_i - 1, face[0, 1:2, :], lane[0:1])
    offs = jnp.where(sub == 0, hi_idx, jnp.where(sub == 7, lo_idx, lane)) - lane
    top = sub < 4
    first_lane, last_lane = lane == 0, lane == 127

    @pl.when(me != 0)
    def _():
        pl.semaphore_wait(barrier, n_i - 1)
        pl.semaphore_signal(joined, inc=1, device_id=dev(w, 0), device_id_type=MESH)

    @pl.when(me == 0)
    def _():
        pl.semaphore_wait(joined, n_i - 1)
        for other in (up_w, dn_w):
            pl.semaphore_signal(barrier, inc=1, device_id=dev(other, 0), device_id_type=MESH)

    def halo(side, i):
        if side == 0:
            row, slot, wheel = (rows * i - 1) % ct, rows + 7, (up_w if i == 0 else w)
            far = i == 0
        else:
            row, slot, wheel = (rows * (i + 1)) % ct, rows, (dn_w if i == n_i - 1 else w)
            far = i == n_i - 1
        src = state.at[:, :, pl.ds(row, 1), :]
        dst = qx.at[mine, :, pl.ds(slot, 1), :]
        remote = pltpu.make_async_remote_copy(
            src, dst, snd_h.at[side, i], rcv_h.at[side, me], device_id=dev(wheel, i), device_id_type=MESH)
        local = pltpu.make_async_copy(src, dst, rcv_h.at[side, me])
        return far, remote, local

    for side in range(2):
        for i in range(n_i):
            far, remote, local = halo(side, i)
            if not far:
                @pl.when(me != i)
                def _(remote=remote):
                    remote.start()

                @pl.when(me == i)
                def _(local=local):
                    local.start()

    def main(off, t):
        to = flip(me, off)
        return pltpu.make_async_remote_copy(
            state.at[:, :, pl.ds(to * rows + 8 * t, 8), :], qx.at[mine, :, pl.ds(8 * t, 8), :],
            snd_m.at[off, t], rcv_m.at[off, t], device_id=dev(w, to), device_id_type=MESH)

    order_out = list(range(2, n_i)) + [1]
    for t in arrivals[:2]:
        for off in order_out:
            main(off, t).start()

    @pl.when(me == 0)
    def _():
        pl.semaphore_wait(barrier, 2)
        for j in range(1, n_i):
            pl.semaphore_signal(around_in, inc=1, device_id=dev(w, j), device_id_type=MESH)

    @pl.when(me != 0)
    def _():
        pl.semaphore_wait(around_in, 1)

    halo(0, 0)[1].start()
    halo(1, n_i - 1)[1].start()
    for t in arrivals[2:]:
        for off in order_out:
            main(off, t).start()
    st_copy.start()

    def tile(buf, n, v, t):
        return buf[n, v, pl.ds(8 * t, 8), :]

    def flux_part(n, q, z):
        both = [jnp.concatenate([q[v], z[v]], axis=0) for v in range(NV)]
        rho, mx, mt, mr, en = both
        inv = 1.0 / rho
        ux, ut = mx * inv, mt * inv
        p = GAMMA1 * (en - 0.5 * (mx * ux + mt * ut + mr * mr * inv))
        h = en + p
        hux = 0.5 * ux[:8]
        hut = 0.5 * ut
        hrel = hut - 0.5 * spd[pl.ds(n, 1), :]
        hp = 0.5 * p
        out = []
        for v in range(NV):
            g = (h[:8] if v == 4 else q[v]) * hux
            f = both[v] * hrel
            if v == 1:
                g = g + hp[:8]
            if v == 2:
                f = f + hp
            if v == 4:
                f = f + p * hut
            a_ax, b_ax = g - q[v], g + q[v]
            right = jnp.where(last_lane, a_ax, shift(a_ax, -1, 1))
            left = jnp.where(first_lane, b_ax, shift(b_ax, 1, 1))
            a_pi, b_pi = f - both[v], f + both[v]
            above = shift(jnp.where(sub == 0, a_pi[8:], a_pi[:8]), -1, 0)
            below = shift(jnp.where(sub == 7, b_pi[8:], b_pi[:8]), 1, 0)
            out.append((left - right) + (below - above) - 4.0 * q[v])
        return out

    def around(buf, n, t, above=True):
        hi = t + 1 if above else t
        lo = tiles if t == 0 else t - 1
        return [jnp.where(top, tile(buf, n, v, hi), tile(buf, n, v, lo)) for v in range(NV)]

    def match(buf):
        @pl.loop(0, inst)
        def _(n):
            for v in range(NV):
                x = tile(buf, n, v, tiles)
                buf[n, v, pl.ds(rows, 8), :] = jnp.where(
                    offs == 0, x, jnp.where(offs == 1, shift(x, -1, 1), shift(x, 1, 1)))

    def section_one(t, above=True):
        @pl.loop(0, NV)
        def _(v):
            q = [tile(qx, n, v, t) for n in range(inst)]
            sp = spectral(q)
            for n in range(inst):
                fx[n, v, pl.ds(8 * t, 8), :] = q[n] - (0.5 * TIME_STEP * FREQUENCY) * sp[n]

        @pl.loop(0, inst, unroll=4)
        def _(n):
            part = flux_part(n, [tile(qx, n, v, t) for v in range(NV)], around(qx, n, t, above))
            for v in range(NV):
                fx[n, v, pl.ds(8 * t, 8), :] += (0.5 * TIME_STEP) * part[v]

    def edges_one():
        def pick(n, v):
            return jnp.where(top, tile(qx, n, v, 0), tile(qx, n, v, tiles - 1))

        @pl.loop(0, NV)
        def _(v):
            q = [pick(n, v) for n in range(inst)]
            sp = spectral(q)
            for n in range(inst):
                eb[n, v] = q[n] - (0.5 * TIME_STEP * FREQUENCY) * sp[n]

        @pl.loop(0, inst, unroll=4)
        def _(n):
            part = flux_part(n, [pick(n, v) for v in range(NV)], [tile(qx, n, v, tiles) for v in range(NV)])
            for v in range(NV):
                eb[n, v] += (0.5 * TIME_STEP) * part[v]

    def section_two(t):
        @pl.loop(0, NV)
        def _(v):
            sp = spectral([tile(fx, n, v, t) for n in range(inst)])
            for n in range(inst):
                rs[n, v, pl.ds(8 * t, 8), :] = -FREQUENCY * sp[n]

        @pl.loop(0, inst, unroll=4)
        def _(n):
            part = flux_part(n, [tile(fx, n, v, t) for v in range(NV)], around(fx, n, t))
            for v in range(NV):
                rs[n, v, pl.ds(8 * t, 8), :] += part[v]

    def back(off, t):
        to = flip(me, off)
        return pltpu.make_async_remote_copy(
            rs.at[pl.ds(to * per, per), :, pl.ds(8 * t, 8), :], res.at[:, :, pl.ds(me * rows + 8 * t, 8), :],
            snd_r.at[off, t], rcv_r.at[off, t], device_id=dev(w, to), device_id_type=MESH)

    def arrive(t):
        for off in range(1, n_i):
            pltpu.make_async_copy(
                state.at[:, :, pl.ds(0, 8), :], qx.at[pl.ds(flip(me, off) * per, per), :, pl.ds(8 * t, 8), :],
                rcv_m.at[off, t]).wait()

    to_above = pltpu.make_async_remote_copy(
        eb.at[:, :, pl.ds(7, 1), :], fx.at[:, :, pl.ds(rows + 7, 1), :], snd_f.at[0], rcv_f.at[0],
        device_id=dev(jnp.where(me == n_i - 1, up_w, w), lax.rem(me + 1, n_i)), device_id_type=MESH)
    to_below = pltpu.make_async_remote_copy(
        eb.at[:, :, pl.ds(0, 1), :], fx.at[:, :, pl.ds(rows, 1), :], snd_f.at[1], rcv_f.at[1],
        device_id=dev(jnp.where(me == 0, dn_w, w), lax.rem(me + n_i - 1, n_i)), device_id_type=MESH)

    own_copy.wait()
    for side in range(2):
        for j in range(n_i):
            dst = qx.at[pl.ds(j * per, per), :, pl.ds(rows if side else rows + 7, 1), :]
            pltpu.make_async_copy(state.at[:, :, pl.ds(0, 1), :], dst, rcv_h.at[side, j]).wait()
    match(qx)
    for t in sorted({0, tiles - 1}):
        arrive(t)
    edges_one()
    to_above.start()
    to_below.start()

    def ghosts():
        to_above.wait_recv()
        to_below.wait_recv()
        match(fx)

    def finish(t):
        section_two(t)
        for off in order_out:
            back(off, t).start()

    if tiles > 3:
        arrive(1)
        section_one(0)
        section_one(1, above=False)
        ghosts()
        finish(0)
        for t in range(2, tiles - 1):
            arrive(t)
        section_one(1)
        for t in range(1, tiles):
            if t + 1 < tiles:
                section_one(t + 1)
            finish(t)
        rest = []
    else:
        for t in range(1, tiles - 1):
            arrive(t)
        for t in range(tiles):
            section_one(t)
        ghosts()
        rest = range(tiles)
    for t in rest:
        finish(t)

    st_copy.wait()
    for t in range(tiles):
        for off in [0, 1] + list(range(2, n_i)):
            j = flip(me, off)
            at = pl.ds(pl.multiple_of(j * rows + 8 * t, 8), 8)
            if off:
                pltpu.make_async_copy(
                    rs.at[mine, :, pl.ds(8 * t, 8), :], res.at[:, :, at, :], rcv_r.at[off, t]).wait()

            for k in range(per):
                for v in range(NV):
                    if off:
                        r = res[k, v, at, :]
                    else:
                        r = rs[me * per + k, v, pl.ds(8 * t, 8), :]
                        res[k, v, at, :] = r
                    new[k, v, at, :] = st[k, v, at, :] + TIME_STEP * r

    for t in range(tiles):
        for off in range(1, n_i):
            main(off, t).wait_send()
            back(off, t).wait_send()
    for side in range(2):
        for i in range(n_i):
            far, remote, local = halo(side, i)
            if far:
                remote.wait_send()
            else:
                @pl.when(me != i)
                def _(remote=remote):
                    remote.wait_send()
    to_above.wait_send()
    to_below.wait_send()


def place(new_v, res_v, new, res, sem):
    copies = []
    for k in range(new_v.shape[0]):
        copies.append(pltpu.make_async_copy(new_v.at[k], new.at[k], sem.at[0, k]))
        copies.append(pltpu.make_async_copy(res_v.at[k], res.at[k], sem.at[1, k]))
    for c in copies:
        c.start()
    for c in copies:
        c.wait()


def body(n_i, n_w, state, slot_blade, blade_class, face_index, amp, phase):
    per, nv, ct, cx = state.shape
    rows = ct // n_i
    tiles = rows // 8
    inst = per * n_i
    dma = pltpu.SemaphoreType.DMA
    anywhere = pl.BlockSpec(memory_space=pl.ANY)
    in_vmem = pl.BlockSpec(memory_space=pltpu.VMEM)

    def stay(x):
        return pltpu.with_memory_space_constraint(x, pltpu.HBM)

    new_v, res_v = pl.pallas_call(
        functools.partial(kernel, n_i, n_w, per, rows),
        out_shape=[pltpu.VMEM(state.shape, jnp.float32)] * 2,
        in_specs=[anywhere] * 6,
        out_specs=[in_vmem] * 2,
        scratch_shapes=[
            pltpu.VMEM(state.shape, jnp.float32),
            pltpu.VMEM((inst, nv, rows + 8, cx), jnp.float32),
            pltpu.VMEM((inst, nv, rows + 8, cx), jnp.float32),
            pltpu.VMEM((inst, nv, 8, cx), jnp.float32),
            pltpu.VMEM((inst, nv, rows, cx), jnp.float32),
            pltpu.VMEM((inst, cx), jnp.float32),
            pltpu.SMEM(slot_blade.shape, jnp.int32),
            pltpu.SMEM(blade_class.shape, jnp.int32),
            pltpu.SMEM(amp.shape, jnp.float32),
            pltpu.SMEM(phase.shape, jnp.float32),
            pltpu.VMEM(face_index.shape, jnp.int32),
            dma((5,)),
            dma((2,)),
            pltpu.SemaphoreType.REGULAR, pltpu.SemaphoreType.REGULAR,
            dma((n_i, tiles)), dma((n_i, tiles)),
            dma((2, n_i)), dma((2, n_i)),
            dma((2,)), dma((2,)),
            dma((n_i, tiles)), dma((n_i, tiles)),
        ],
        compiler_params=pltpu.CompilerParams(
            collective_id=0, has_side_effects=True, vmem_limit_bytes=32 * 1024 * 1024),
        cost_estimate=pl.CostEstimate(flops=50_000_000, bytes_accessed=2_700_000, transcendentals=0),
    )(stay(state), slot_blade, stay(blade_class), stay(amp), stay(phase), stay(face_index))
    return pl.pallas_call(
        place,
        out_shape=[jax.ShapeDtypeStruct(state.shape, jnp.float32)] * 2,
        in_specs=[anywhere] * 2,
        out_specs=[anywhere] * 2,
        scratch_shapes=[dma((2, per))],
        cost_estimate=pl.CostEstimate(flops=0, bytes_accessed=5_200_000, transcendentals=0),
    )(*[pltpu.with_memory_space_constraint(x, pltpu.VMEM) for x in (new_v, res_v)])


def solution(mesh):
    placed = (
        P("inst", None, ("cases", "wheel"), None),
        P(("cases", "wheel")),
        P("cases"),
        P(("cases", "wheel"), None, None),
        P(),
        P(),
    )
    return jax.shard_map(
        functools.partial(body, mesh.shape["inst"], mesh.shape["wheel"]),
        mesh=mesh,
        in_specs=placed,
        out_specs=(
            P("inst", None, ("cases", "wheel"), None),
            P("inst", None, ("cases", "wheel"), None),
        ),
        check_vma=False,
    )
```

```python
import functools
import math

import jax
import jax.numpy as jnp
from jax import lax
from jax.experimental import pallas as pl
from jax.experimental.pallas import tpu as pltpu
from jax.sharding import PartitionSpec as P

TIME_STEP = 0.05
GAMMA1 = 0.4
FREQUENCY = 0.5
NV = 5
MESH = pl.DeviceIdType.MESH


def flip(i, off):
    out, b = i, 1
    while b <= off:
        if off & b:
            out = out + b - 2 * b * ((i // b) % 2)
        b *= 2
    return out


def spectral(q):
    s = [q[i] + q[i + 8] for i in range(8)]
    d = [q[i] - q[i + 8] for i in range(8)]
    c = [0.5 * (-1) ** k / math.tan(math.pi * k / 8) for k in range(1, 4)]
    t = [0.5 * (-1) ** k / math.sin(math.pi * k / 8) for k in range(1, 4)]
    s2 = [s[i] - s[(i + 2) % 8] for i in range(8)]
    s4 = [s[i] - s[i + 4] for i in range(4)]

    def dd(i):
        i %= 16
        return (d[i], 1) if i < 8 else (d[i - 8], -1)

    cache = {}

    def ddiff(i, j):
        (x, sx), (y, sy) = dd(i), dd(j)
        key = (i % 8, j % 8, sx * sy)
        if key not in cache:
            cache[key] = x - y if sx * sy > 0 else x + y
        return cache[key], sx

    out = [None] * 16
    for n in range(8):
        a1 = s2[(n - 1) % 8]
        a3 = s2[(n + 3) % 8]
        i = (n - 2) % 8
        a2 = s4[i] * c[1] if i < 4 else s4[i - 4] * (-c[1])
        u = c[0] * a1 - c[2] * a3 + a2
        w = None
        for k in (1, 2, 3):
            v, sg = ddiff(n - k, n + k)
            term = v * (sg * t[k - 1])
            w = term if w is None else w + term
        x, sg = dd(n - 4)
        w = w + x * (0.5 * sg)
        out[n] = u + w
        out[n + 8] = u - w
    return out


def shift(x, k, axis):
    size = x.shape[axis]
    return pltpu.roll(x, k % size, axis)


def kernel(n_i, n_w, per, rows, state, slot_blade_h, blade_class_h, amp_h, phase_h, face_h, new, res,
           st, qx, fx, rs, spd, slot_blade, blade_class, amp, phase, face, par_sem, own_sem,
           joined, around_in, snd_m, rcv_m, snd_h, rcv_h, snd_f, rcv_f, snd_r, rcv_r):
    me = lax.axis_index("inst")
    w = lax.axis_index("wheel")
    up_w, dn_w = lax.rem(w + 1, n_w), lax.rem(w + n_w - 1, n_w)
    ct = rows * n_i
    inst = n_i * per
    tiles = rows // 8
    def dev(wheel, i):
        return {"wheel": wheel, "inst": i}

    small = [(slot_blade_h, slot_blade), (blade_class_h, blade_class), (amp_h, amp), (phase_h, phase), (face_h, face)]
    for i, (a, b) in enumerate(small):
        pltpu.make_async_copy(a, b, par_sem.at[i]).start()

    barrier = pltpu.get_barrier_semaphore()

    @pl.when(me == 0)
    def _():
        for j in range(1, n_i):
            pl.semaphore_signal(barrier, inc=1, device_id=dev(w, j), device_id_type=MESH)

    @pl.when(me != 0)
    def _():
        for j in range(1, n_i):
            @pl.when(me != j)
            def _(j=j):
                pl.semaphore_signal(barrier, inc=1, device_id=dev(w, j), device_id_type=MESH)

    mine = pl.ds(me * per, per)
    own_copy = pltpu.make_async_copy(
        state.at[:, :, pl.ds(me * rows, rows), :], qx.at[mine, :, pl.ds(0, rows), :], own_sem.at[0])
    own_copy.start()
    st_copy = pltpu.make_async_copy(state, st, own_sem.at[1])
    @pl.when(me != 0)
    def _():
        pl.semaphore_wait(barrier, n_i - 1)
        pl.semaphore_signal(joined, inc=1, device_id=dev(w, 0), device_id_type=MESH)

    @pl.when(me == 0)
    def _():
        pl.semaphore_wait(joined, n_i - 1)
        for other in (up_w, dn_w):
            pl.semaphore_signal(barrier, inc=1, device_id=dev(other, 0), device_id_type=MESH)

    def halo(side, i):
        if side == 0:
            row, slot, wheel = (rows * i - 1) % ct, rows + 7, (up_w if i == 0 else w)
            far = i == 0
        else:
            row, slot, wheel = (rows * (i + 1)) % ct, rows, (dn_w if i == n_i - 1 else w)
            far = i == n_i - 1
        src = state.at[:, :, pl.ds(row, 1), :]
        dst = qx.at[mine, :, pl.ds(slot, 1), :]
        remote = pltpu.make_async_remote_copy(
            src, dst, snd_h.at[side, i], rcv_h.at[side, me], device_id=dev(wheel, i), device_id_type=MESH)
        local = pltpu.make_async_copy(src, dst, rcv_h.at[side, me])
        return far, remote, local

    for side in range(2):
        for i in range(n_i):
            far, remote, local = halo(side, i)
            if not far:
                @pl.when(me != i)
                def _(remote=remote):
                    remote.start()

                @pl.when(me == i)
                def _(local=local):
                    local.start()

    def main(off, t):
        to = flip(me, off)
        return pltpu.make_async_remote_copy(
            state.at[:, :, pl.ds(to * rows + 8 * t, 8), :], qx.at[mine, :, pl.ds(8 * t, 8), :],
            snd_m.at[off, t], rcv_m.at[off, t], device_id=dev(w, to), device_id_type=MESH)

    order_out = list(range(2, n_i)) + [1]
    for t in range(min(2, tiles)):
        for off in order_out:
            main(off, t).start()

    @pl.when(me == 0)
    def _():
        pl.semaphore_wait(barrier, 2)
        for j in range(1, n_i):
            pl.semaphore_signal(around_in, inc=1, device_id=dev(w, j), device_id_type=MESH)

    @pl.when(me != 0)
    def _():
        pl.semaphore_wait(around_in, 1)

    halo(0, 0)[1].start()
    halo(1, n_i - 1)[1].start()
    for t in range(2, tiles):
        for off in order_out:
            main(off, t).start()
    st_copy.start()

    for i, (a, b) in enumerate(small):
        pltpu.make_async_copy(a, b, par_sem.at[i]).wait()
    cls = blade_class[slot_blade[0]]
    instance = lax.broadcasted_iota(jnp.int32, (inst, 128), 0).astype(jnp.float32)
    spd[...] = amp[cls] * jnp.sin((2.0 * math.pi / inst) * instance + phase[cls])
    lane = lax.broadcasted_iota(jnp.int32, (8, 128), 1)
    sub = lax.broadcasted_iota(jnp.int32, (8, 128), 0)
    lo_idx = jnp.where(me == 0, face[0, 0:1, :], lane[0:1])
    hi_idx = jnp.where(me == n_i - 1, face[0, 1:2, :], lane[0:1])
    offs = jnp.where(sub == 0, hi_idx, jnp.where(sub == 7, lo_idx, lane)) - lane
    top = sub < 4
    first_lane, last_lane = lane == 0, lane == 127

    def tile(buf, n, v, t):
        return buf[n, v, pl.ds(8 * t, 8), :]

    def flux_part(n, q, z):
        both = [jnp.concatenate([q[v], z[v]], axis=0) for v in range(NV)]
        rho, mx, mt, mr, en = both
        inv = 1.0 / rho
        ux, ut = mx * inv, mt * inv
        p = GAMMA1 * (en - 0.5 * (mx * ux + mt * ut + mr * mr * inv))
        h = en + p
        hux = 0.5 * ux[:8]
        hut = 0.5 * ut
        hrel = hut - 0.5 * spd[pl.ds(n, 1), :]
        hp = 0.5 * p
        out = []
        for v in range(NV):
            g = (h[:8] if v == 4 else q[v]) * hux
            f = both[v] * hrel
            if v == 1:
                g = g + hp[:8]
            if v == 2:
                f = f + hp
            if v == 4:
                f = f + p * hut
            a_ax, b_ax = g - q[v], g + q[v]
            right = jnp.where(last_lane, a_ax, shift(a_ax, -1, 1))
            left = jnp.where(first_lane, b_ax, shift(b_ax, 1, 1))
            a_pi, b_pi = f - both[v], f + both[v]
            above = shift(jnp.where(sub == 0, a_pi[8:], a_pi[:8]), -1, 0)
            below = shift(jnp.where(sub == 7, b_pi[8:], b_pi[:8]), 1, 0)
            out.append((left - right) + (below - above) - 4.0 * q[v])
        return out

    def around(buf, n, t, above=True):
        hi = t + 1 if above else t
        lo = tiles if t == 0 else t - 1
        return [jnp.where(top, tile(buf, n, v, hi), tile(buf, n, v, lo)) for v in range(NV)]

    def match(buf):
        @pl.loop(0, inst, unroll=4)
        def _(n):
            for v in range(NV):
                x = tile(buf, n, v, tiles)
                buf[n, v, pl.ds(rows, 8), :] = jnp.where(
                    offs == 0, x, jnp.where(offs == 1, shift(x, -1, 1), shift(x, 1, 1)))

    def section_one(t, above=True):
        @pl.loop(0, NV)
        def _(v):
            q = [tile(qx, n, v, t) for n in range(inst)]
            sp = spectral(q)
            for n in range(inst):
                fx[n, v, pl.ds(8 * t, 8), :] = q[n] - (0.5 * TIME_STEP * FREQUENCY) * sp[n]

        @pl.loop(0, inst, unroll=4)
        def _(n):
            part = flux_part(n, [tile(qx, n, v, t) for v in range(NV)], around(qx, n, t, above))
            for v in range(NV):
                fx[n, v, pl.ds(8 * t, 8), :] += (0.5 * TIME_STEP) * part[v]

    def section_two(t):
        @pl.loop(0, NV)
        def _(v):
            sp = spectral([tile(fx, n, v, t) for n in range(inst)])
            for n in range(inst):
                rs[n, v, pl.ds(8 * t, 8), :] = -FREQUENCY * sp[n]

        @pl.loop(0, inst, unroll=4)
        def _(n):
            part = flux_part(n, [tile(fx, n, v, t) for v in range(NV)], around(fx, n, t))
            for v in range(NV):
                rs[n, v, pl.ds(8 * t, 8), :] += part[v]

    def back(off, t):
        to = flip(me, off)
        return pltpu.make_async_remote_copy(
            rs.at[pl.ds(to * per, per), :, pl.ds(8 * t, 8), :], res.at[:, :, pl.ds(me * rows + 8 * t, 8), :],
            snd_r.at[off, t], rcv_r.at[off, t], device_id=dev(w, to), device_id_type=MESH)

    def arrive(t):
        for off in range(1, n_i):
            pltpu.make_async_copy(
                state.at[:, :, pl.ds(0, 8), :], qx.at[pl.ds(flip(me, off) * per, per), :, pl.ds(8 * t, 8), :],
                rcv_m.at[off, t]).wait()

    to_above = pltpu.make_async_remote_copy(
        fx.at[:, :, pl.ds(rows - 1, 1), :], fx.at[:, :, pl.ds(rows + 7, 1), :], snd_f.at[0], rcv_f.at[0],
        device_id=dev(jnp.where(me == n_i - 1, up_w, w), lax.rem(me + 1, n_i)), device_id_type=MESH)
    to_below = pltpu.make_async_remote_copy(
        fx.at[:, :, pl.ds(0, 1), :], fx.at[:, :, pl.ds(rows, 1), :], snd_f.at[1], rcv_f.at[1],
        device_id=dev(jnp.where(me == 0, dn_w, w), lax.rem(me + n_i - 1, n_i)), device_id_type=MESH)

    own_copy.wait()
    for side in range(2):
        for j in range(n_i):
            dst = qx.at[pl.ds(j * per, per), :, pl.ds(rows if side else rows + 7, 1), :]
            pltpu.make_async_copy(state.at[:, :, pl.ds(0, 1), :], dst, rcv_h.at[side, j]).wait()
    match(qx)
    def ghosts():
        to_above.wait_recv()
        to_below.wait_recv()
        match(fx)

    def finish(t):
        section_two(t)
        for off in order_out:
            back(off, t).start()

    if tiles > 3:
        arrive(0)
        arrive(1)
        section_one(0)
        to_below.start()
        for t in range(1, tiles - 2):
            arrive(t + 1)
            section_one(t)
        section_one(tiles - 2, above=False)
        for t in range(1, tiles - 2):
            finish(t)
        arrive(tiles - 1)
        section_one(tiles - 1)
        to_above.start()
        section_one(tiles - 2)
        finish(tiles - 2)
        ghosts()
        finish(0)
        finish(tiles - 1)
        returns = list(range(1, tiles - 1)) + [0, tiles - 1]
    else:
        for t in range(tiles):
            arrive(t)
        for t in range(tiles):
            section_one(t)
        to_below.start()
        to_above.start()
        ghosts()
        for t in range(tiles):
            finish(t)
        returns = list(range(tiles))

    st_copy.wait()
    for t in returns:
        for off in [0, 1] + list(range(2, n_i)):
            j = flip(me, off)
            at = pl.ds(pl.multiple_of(j * rows + 8 * t, 8), 8)
            if off:
                pltpu.make_async_copy(
                    rs.at[mine, :, pl.ds(8 * t, 8), :], res.at[:, :, at, :], rcv_r.at[off, t]).wait()

            for k in range(per):
                for v in range(NV):
                    if off:
                        r = res[k, v, at, :]
                    else:
                        r = rs[me * per + k, v, pl.ds(8 * t, 8), :]
                        res[k, v, at, :] = r
                    new[k, v, at, :] = st[k, v, at, :] + TIME_STEP * r

    for t in range(tiles):
        for off in range(1, n_i):
            main(off, t).wait_send()
            back(off, t).wait_send()
    for side in range(2):
        for i in range(n_i):
            far, remote, local = halo(side, i)
            if far:
                remote.wait_send()
            else:
                @pl.when(me != i)
                def _(remote=remote):
                    remote.wait_send()
    to_above.wait_send()
    to_below.wait_send()


def place(new_v, res_v, new, res, sem):
    copies = []
    for k in range(new_v.shape[0]):
        copies.append(pltpu.make_async_copy(new_v.at[k], new.at[k], sem.at[0, k]))
        copies.append(pltpu.make_async_copy(res_v.at[k], res.at[k], sem.at[1, k]))
    for c in copies:
        c.start()
    for c in copies:
        c.wait()


def body(n_i, n_w, state, slot_blade, blade_class, face_index, amp, phase):
    per, nv, ct, cx = state.shape
    rows = ct // n_i
    tiles = rows // 8
    inst = per * n_i
    dma = pltpu.SemaphoreType.DMA
    anywhere = pl.BlockSpec(memory_space=pl.ANY)
    in_vmem = pl.BlockSpec(memory_space=pltpu.VMEM)

    def stay(x):
        return pltpu.with_memory_space_constraint(x, pltpu.HBM)

    new_v, res_v = pl.pallas_call(
        functools.partial(kernel, n_i, n_w, per, rows),
        out_shape=[pltpu.VMEM(state.shape, jnp.float32)] * 2,
        in_specs=[anywhere] * 6,
        out_specs=[in_vmem] * 2,
        scratch_shapes=[
            pltpu.VMEM(state.shape, jnp.float32),
            pltpu.VMEM((inst, nv, rows + 8, cx), jnp.float32),
            pltpu.VMEM((inst, nv, rows + 8, cx), jnp.float32),
            pltpu.VMEM((inst, nv, rows, cx), jnp.float32),
            pltpu.VMEM((inst, cx), jnp.float32),
            pltpu.SMEM(slot_blade.shape, jnp.int32),
            pltpu.SMEM(blade_class.shape, jnp.int32),
            pltpu.SMEM(amp.shape, jnp.float32),
            pltpu.SMEM(phase.shape, jnp.float32),
            pltpu.VMEM(face_index.shape, jnp.int32),
            dma((5,)),
            dma((2,)),
            pltpu.SemaphoreType.REGULAR, pltpu.SemaphoreType.REGULAR,
            dma((n_i, tiles)), dma((n_i, tiles)),
            dma((2, n_i)), dma((2, n_i)),
            dma((2,)), dma((2,)),
            dma((n_i, tiles)), dma((n_i, tiles)),
        ],
        compiler_params=pltpu.CompilerParams(
            collective_id=0, has_side_effects=True, vmem_limit_bytes=32 * 1024 * 1024),
        cost_estimate=pl.CostEstimate(flops=50_000_000, bytes_accessed=2_700_000, transcendentals=0),
    )(stay(state), slot_blade, stay(blade_class), stay(amp), stay(phase), stay(face_index))
    return pl.pallas_call(
        place,
        out_shape=[jax.ShapeDtypeStruct(state.shape, jnp.float32)] * 2,
        in_specs=[anywhere] * 2,
        out_specs=[anywhere] * 2,
        scratch_shapes=[dma((2, per))],
        cost_estimate=pl.CostEstimate(flops=0, bytes_accessed=5_200_000, transcendentals=0),
    )(*[pltpu.with_memory_space_constraint(x, pltpu.VMEM) for x in (new_v, res_v)])


def solution(mesh):
    placed = (
        P("inst", None, ("cases", "wheel"), None),
        P(("cases", "wheel")),
        P("cases"),
        P(("cases", "wheel"), None, None),
        P(),
        P(),
    )
    return jax.shard_map(
        functools.partial(body, mesh.shape["inst"], mesh.shape["wheel"]),
        mesh=mesh,
        in_specs=placed,
        out_specs=(
            P("inst", None, ("cases", "wheel"), None),
            P("inst", None, ("cases", "wheel"), None),
        ),
        check_vma=False,
    )
```
